256 devices in a mesh: fsdp: 128 (over y, x_lo, z, core), seq: 2 (over x_hi).
Axes of the slice: x: 4 (x_hi: 2, x_lo: 2; x = x_hi * 2 + x_lo), y: 4, z: 8, core: 2. Of those that a mesh axis runs over, the one named last changes fastest.
Arguments:
- tokens: bfloat16 [16384, 8192], P('fsdp', 'seq'), may hold values from -6 to 6
- weight: bfloat16 [1024, 8192], P('fsdp', 'seq'), may hold values from -0.0625 to 0.0625
- bias: float32 [1024], P('seq'), may hold values from -3 to 3
- adapter_down: bfloat16 [8192, 512, 64], P('seq', 'fsdp'), may hold values from -0.0625 to 0.0625
- adapter_up: bfloat16 [512, 64, 1024], P('fsdp', None, 'seq'), may hold values from -0.75 to 0.75
- cotangent: bfloat16 [16384, 1024], P('fsdp', 'seq'), may hold values from -6 to 6
- block_task: int32 [8192], P('fsdp'), may hold values from 0 to 511, as said below
- owner_slot: int32 [512], replicated, may hold values from 0 to 511, as said below
Outputs:
- projected: bfloat16 [16384, 1024], P('fsdp', 'seq')
- grad_tokens: bfloat16 [16384, 8192], P('fsdp', 'seq')
- down_gradient: float32 [8192, 512, 64], P('seq', 'fsdp')
- up_gradient: float32 [512, 64, 1024], P('fsdp', None, 'seq')
The draws below stay inside these ranges and needn't reach their ends.
Inputs may be any that keep to these rules, and one draw needn't show every extreme that they name: `block_task`: within one index of fsdp (aligned runs of 64 entries) the blocks name tasks whose owner devices owner_slot[task] // 4 all differ. `owner_slot`: A permutation; slot s is held by index s // 4 of fsdp.
All inputs are finite; a program needn't handle non-finite values.
Results may differ from the reference program's by a relative error of at most 0.0036.
Values may be sent and summed in bfloat16 or wider, within the bound.
No kernel may reach another device: no remote copies, remote signals or barrier semaphores. Data moves between devices by JAX's collectives and lax.ppermute only.
A program may use at most 128 MiB of HBM per device.

```python
import jax
import jax.numpy as jnp
from jax import lax

D = 8192
KEY_FEATURES = 1024
R = 64
TASK_DEV = 4
BLK_DEV = 64
BLK = 2
TASKS = 512
TOKEN_TOTAL = 16384


def shared_slots(key):
    return jax.random.permutation(jax.random.fold_in(key, 11), TASKS).astype(jnp.int32)


def draw_owner_slot(key, part):
    slot_map = shared_slots(key)
    return slot_map


def draw_block_task(key, part):
    slot_map = shared_slots(key)
    key = jax.random.fold_in(key, 2)
    owning_count = TASKS // TASK_DEV
    subkeys = jax.random.split(key, 5)
    hottest = jax.random.randint(subkeys[0], (), 0, owning_count)
    popular = jax.random.randint(subkeys[1], (owning_count,), 0, 8)
    jitter = jax.random.randint(subkeys[2], (owning_count, owning_count), 0, 65536)
    owners = jnp.arange(owning_count, dtype=jnp.int32)
    scores = jitter + popular[None, :] * 8192 + jnp.where(owners == hottest, 262144, 0)[None, :]
    scores = scores * owning_count + owners[None, :]
    _, picked = lax.top_k(scores, BLK_DEV)
    shuffled = jax.vmap(jax.random.permutation)(jax.random.split(subkeys[3], owning_count), picked)
    inner_slot = jax.random.randint(subkeys[4], (owning_count, BLK_DEV), 0, TASK_DEV)
    wanted = shuffled * TASK_DEV + inner_slot
    inverse = jnp.argsort(slot_map, stable=True).astype(jnp.int32)
    return inverse[wanted].reshape(owning_count * BLK_DEV).astype(jnp.int32)


def block_levels(own_key, shape, pieces, low, top_value):
    gain, own = 1.0, jax.random.fold_in(own_key, 6)
    for dim, shards_of in pieces:
        draws = jnp.exp(jax.random.uniform(jax.random.fold_in(own, dim), (shards_of,), jnp.float32, low / len(pieces), top_value / len(pieces)))
        gain = gain * jnp.repeat(draws, shape[dim] // shards_of).reshape([-1 if axis == dim else 1 for axis in range(len(shape))])
    return gain


def bell_draw(stream_key, dims, deviation, bound, cuts=(), kind=jnp.bfloat16):
    array = jax.random.normal(stream_key, dims, jnp.float32) * deviation
    if len(cuts) > 0:
        array = block_levels(stream_key, dims, cuts, -0.22, 0.18) * array
    return jnp.clip(array, min=-bound, max=bound).astype(kind)


def setup_inputs(seed: int = 0) -> dict:
    seeds = jax.random.split(jax.random.key(seed), 9)
    tokens = bell_draw(seeds[0], (TOKEN_TOTAL, D), 1.0, 6.0, ((0, 128), (1, 2)))
    weight = bell_draw(seeds[1], (KEY_FEATURES, D), D ** -0.5, 0.0625, ((0, 128), (1, 2)))
    bias = bell_draw(seeds[2], (KEY_FEATURES,), 0.5, 3.0, ((0, 2),), jnp.float32)
    adapter_down = bell_draw(seeds[3], (D, TASKS, R), D ** -0.5, 0.0625, ((0, 2), (1, 128)))
    adapter_up = bell_draw(seeds[4], (TASKS, R, KEY_FEATURES), R ** -0.5, 0.75, ((0, 128), (2, 2)))
    cotangent = bell_draw(seeds[5], (TOKEN_TOTAL, KEY_FEATURES), 1.0, 6.0, ((0, 128), (1, 2)))
    block_task = draw_block_task(jax.random.fold_in(seeds[8], 71), 0)
    owner_slot = draw_owner_slot(jax.random.fold_in(seeds[8], 71), 0)
    return {"tokens": tokens, "weight": weight, "bias": bias, "adapter_down": adapter_down, "adapter_up": adapter_up, "cotangent": cotangent, "block_task": block_task, "owner_slot": owner_slot}


adapter_scale = 0.5


def reference(tokens, weight, bias, adapter_down, adapter_up, cotangent, block_task, owner_slot):
    match_task = block_task[:, None] == jnp.arange(TASKS, dtype=jnp.int32)[None, :]
    task_positions = jnp.sum(jnp.where(match_task, owner_slot[None, :], 0), axis=1).astype(jnp.int32)
    token_block_rows = tokens.reshape(-1, BLK, D)
    gradient_per_block = cotangent.reshape(-1, BLK, KEY_FEATURES)

    def single_block(carry, item):
        down_sum_total, up_sum_total = carry
        block_rows, per_block_gradient, slot = item
        down_map = lax.dynamic_index_in_dim(adapter_down, slot, 1, keepdims=False)
        up_weight_mapping = lax.dynamic_index_in_dim(adapter_up, slot, 0, keepdims=False)
        reduced_input = jnp.dot(block_rows, down_map, preferred_element_type=jnp.float32).astype(jnp.bfloat16)
        adapter_output = (adapter_scale * jnp.dot(reduced_input, up_weight_mapping, preferred_element_type=jnp.float32)).astype(jnp.bfloat16)
        reduced_gradient = (adapter_scale * jnp.dot(per_block_gradient, up_weight_mapping.T, preferred_element_type=jnp.float32)).astype(jnp.bfloat16)
        down_term = jnp.dot(block_rows.T, reduced_gradient, preferred_element_type=jnp.float32)
        up_weight_term = adapter_scale * jnp.dot(reduced_input.T, per_block_gradient, preferred_element_type=jnp.float32)
        zero_index = jnp.zeros((), jnp.int32)
        old_down = lax.dynamic_slice(down_sum_total, (zero_index, slot, zero_index), (D, 1, R))
        down_sum_total = lax.dynamic_update_slice(down_sum_total, old_down + down_term[:, None, :], (zero_index, slot, zero_index))
        old_up = lax.dynamic_slice(up_sum_total, (slot, zero_index, zero_index), (1, R, KEY_FEATURES))
        up_sum_total = lax.dynamic_update_slice(up_sum_total, old_up + up_weight_term[None, :, :], (slot, zero_index, zero_index))
        returned_rows = jnp.dot(reduced_gradient, down_map.T, preferred_element_type=jnp.float32).astype(jnp.bfloat16)
        return (down_sum_total, up_sum_total), (adapter_output, returned_rows)

    start_index = (jnp.zeros((D, TASKS, R), jnp.float32), jnp.zeros((TASKS, R, KEY_FEATURES), jnp.float32))
    (down_gradient, up_gradient), (adapter_output_rows, backward_outputs) = lax.scan(single_block, start_index, (token_block_rows, gradient_per_block, task_positions))
    frozen_product = jnp.dot(tokens, weight.T, preferred_element_type=jnp.float32) + bias
    projected = (frozen_product + adapter_output_rows.reshape(TOKEN_TOTAL, KEY_FEATURES).astype(jnp.float32)).astype(jnp.bfloat16)
    base_grad = jnp.dot(cotangent, weight, preferred_element_type=jnp.float32)
    grad_tokens = (base_grad + backward_outputs.reshape(TOKEN_TOTAL, D).astype(jnp.float32)).astype(jnp.bfloat16)
    return (projected, grad_tokens, down_gradient, up_gradient)
```

```python
import jax
import jax.numpy as jnp
from jax import lax
from jax.experimental import pallas as pl
from jax.experimental.pallas import tpu as pltpu
from jax.sharding import Mesh, PartitionSpec as P

adapter_scale = 0.5
GROUPS = 4
SUB = ("y", "xl", "z", "c")
SPLIT = (4, 2, 8, 2)
bf16 = jnp.bfloat16
f32 = jnp.float32
VMEM = pl.BlockSpec(memory_space=pltpu.VMEM)
PARAMS = pltpu.CompilerParams(vmem_limit_bytes=48 * 1024 * 1024)


def dot(a, b, da=1, db=0):
    return lax.dot_general(a, b, (((da,), (db,)), ((), ())), preferred_element_type=f32)


def iota(shape, dim):
    return lax.broadcasted_iota(jnp.int32, shape, dim)


def pack_kernel(key_ref, label_ref, tok_ref, cot_ref, out_ref, stack):
    rows, width = tok_ref.shape
    tw, cw = width // GROUPS, cot_ref.shape[1] // GROUPS
    for g in range(GROUPS):
        stack[g * rows:(g + 1) * rows, :tw] = tok_ref[:, g * tw:(g + 1) * tw]
        stack[g * rows:(g + 1) * rows, tw:] = cot_ref[:, g * cw:(g + 1) * cw]
    total = out_ref.shape[0]
    step = 256
    for b in range(total // step):
        part = slice(b * step, (b + 1) * step)
        pick = (key_ref[part, :] == iota((step, GROUPS * rows), 1)).astype(f32).astype(bf16)
        out_ref[part, :tw + cw] = dot(pick, stack[...]).astype(bf16)
        out_ref[part, tw + cw:] = jnp.broadcast_to(label_ref[part, :], (step, 128)).astype(bf16)


def order(chunk, groups):
    out, src = iota((chunk, chunk), 0), iota((chunk, chunk), 1)
    per = chunk // groups
    return (src == (out % per) * groups + out // per).astype(f32).astype(bf16)


def reorder(chunk, groups):
    src, out = iota((chunk, chunk), 1), iota((chunk, chunk), 0)
    per = chunk // groups
    return (out == (src % per) * groups + src // per).astype(f32).astype(bf16)


def collapse(part, label, tasks, rank):
    total = jnp.zeros((part.shape[0], rank), f32)
    for j in range(tasks):
        total = total + jnp.where(label == j, part[:, j * rank:(j + 1) * rank], 0.0)
    return total


def spread(low, label, tasks):
    return jnp.concatenate(
        [jnp.where(label == j, low, 0.0) for j in range(tasks)], axis=1
    ).astype(bf16)


def owner_in_kernel(tasks, got_ref, down_ref, up_ref, low_ref, rows_ref, cots_ref, label_ref):
    width = down_ref.shape[1]
    key_part = up_ref.shape[1]
    rank = down_ref.shape[0] // tasks
    tw, cw = width // GROUPS, key_part // GROUPS
    step = 256
    per = step // GROUPS
    to_rows = order(step, GROUPS)
    for b in range(got_ref.shape[0] // step):
        block = dot(to_rows, got_ref[b * step:(b + 1) * step, :]).astype(bf16)
        at = slice(b * per, (b + 1) * per)
        for g in range(GROUPS):
            piece = block[g * per:(g + 1) * per, :]
            rows_ref[at, g * tw:(g + 1) * tw] = piece[:, :tw]
            cots_ref[at, g * cw:(g + 1) * cw] = piece[:, tw:tw + cw]
        label_ref[at, :] = block[:per, tw + cw:]
    label = label_ref[...].astype(f32)[:, :rank]
    low_ref[:, :rank] = collapse(dot(rows_ref[...], down_ref[...], 1, 1), label, tasks, rank)
    low_ref[:, rank:] = collapse(dot(cots_ref[...], up_ref[...], 1, 1), label, tasks, rank)


def owner_out_kernel(tasks, mine_ref, other_ref, label_ref, down_ref, up_ref, out_ref, low_ref, grad_ref, back, lora):
    rank = down_ref.shape[0] // tasks
    width, key_part = down_ref.shape[1], up_ref.shape[1]
    tw, cw = width // GROUPS, key_part // GROUPS
    total = mine_ref[...] + other_ref[...]
    label = label_ref[...].astype(f32)[:, :rank]
    low = total[:, :rank].astype(bf16).astype(f32)
    grad = (adapter_scale * total[:, rank:]).astype(bf16).astype(f32)
    low_wide = spread(low, label, tasks)
    grad_wide = spread(grad, label, tasks)
    low_ref[...] = low_wide
    grad_ref[...] = grad_wide
    lora[...] = (adapter_scale * dot(low_wide, up_ref[...])).astype(bf16)
    for g in range(GROUPS):
        cols = slice(g * tw, (g + 1) * tw)
        back[:, cols] = dot(grad_wide, down_ref[:, cols]).astype(bf16)
    step = 256
    per = step // GROUPS
    to_sent = reorder(step, GROUPS)
    for b in range(out_ref.shape[0] // step):
        at = slice(b * per, (b + 1) * per)
        rows = jnp.concatenate([back[at, g * tw:(g + 1) * tw] for g in range(GROUPS)], axis=0)
        adds = jnp.concatenate([lora[at, g * cw:(g + 1) * cw] for g in range(GROUPS)], axis=0)
        where = slice(b * step, (b + 1) * step)
        out_ref[where, :tw] = dot(to_sent, rows).astype(bf16)
        out_ref[where, tw:] = dot(to_sent, adds).astype(bf16)


def finish_kernel(key_ref, got_ref, base_ref, frozen_ref, bias_ref, grad_ref, proj_ref):
    rows, width = grad_ref.shape
    key_part = proj_ref.shape[1]
    tw, cw = width // GROUPS, key_part // GROUPS
    total = got_ref.shape[0]
    for g in range(GROUPS):
        pick = (key_ref[...] + g == iota((rows, total), 1)).astype(f32).astype(bf16)
        cols, keys = slice(g * tw, (g + 1) * tw), slice(g * cw, (g + 1) * cw)
        grad_ref[:, cols] = (base_ref[:, cols] + dot(pick, got_ref[:, :tw])).astype(bf16)
        proj_ref[:, keys] = (
            frozen_ref[:, keys] + bias_ref[:, keys] + dot(pick, got_ref[:, tw:])
        ).astype(bf16)


def swap(value, axis):
    return lax.ppermute(value, axis, [(0, 1), (1, 0)])


def on_device(tokens, weight, bias, adapter_down, adapter_up, cotangent, block_task, owner_slot):
    rows_dev, half_width = tokens.shape
    owners = SPLIT[0] * SPLIT[1] * SPLIT[2] * SPLIT[3]
    blocks_dev = block_task.shape[0]
    block_rows = rows_dev // blocks_dev
    task_dev, rank, key_part = adapter_up.shape
    tasks_all = owner_slot.shape[0]
    chunk = block_rows * GROUPS
    sent_rows = owners * chunk
    tw, cw = half_width // GROUPS, key_part // GROUPS
    seq = lax.axis_index("seq")
    core = lax.axis_index("c")

    match_task = block_task[:, None] == jnp.arange(tasks_all, dtype=jnp.int32)[None, :]
    slot_of = jnp.sum(jnp.where(match_task, owner_slot[None, :], 0), axis=1)
    owner_of = slot_of // task_dev
    inner_of = slot_of % task_dev
    owner_row = jnp.arange(sent_rows, dtype=jnp.int32) // chunk
    match_owner = owner_of[None, :] == owner_row[:, None]
    block_pick = jnp.sum(
        jnp.where(match_owner, jnp.arange(blocks_dev, dtype=jnp.int32)[None, :] + 1, 0), axis=1
    )
    label = jnp.sum(jnp.where(match_owner, inner_of[None, :] + 1, 0), axis=1) - 1
    within = jnp.arange(sent_rows, dtype=jnp.int32) % chunk
    key = jnp.where(
        block_pick > 0,
        (block_pick - 1) * block_rows + within // GROUPS + (within % GROUPS) * rows_dev,
        -1,
    )
    sent = pl.pallas_call(
        pack_kernel,
        out_shape=jax.ShapeDtypeStruct((sent_rows, tw + cw + 128), bf16),
        in_specs=[VMEM] * 4,
        out_specs=VMEM,
        scratch_shapes=[pltpu.VMEM((GROUPS * rows_dev, tw + cw), bf16)],
        compiler_params=PARAMS,
        name="pack",
    )(key[:, None], label.astype(f32)[:, None], tokens, cotangent)
    got = lax.all_to_all(sent, SUB, split_axis=0, concat_axis=0, tiled=True)

    stage = lax.all_gather(weight, "xl", axis=0)
    stage = lax.all_gather(stage, "z", axis=0)
    stage = lax.all_gather(stage, "y", axis=0)
    own_weight = stage.reshape(-1, half_width)
    other_weight = swap(own_weight, "c")

    down_t = adapter_down.transpose(1, 2, 0).reshape(task_dev * rank, half_width)
    up_t = adapter_up.reshape(task_dev * rank, key_part)
    owner_rows = owners * block_rows
    low_mine, rows_in, cots_in, label_in = pl.pallas_call(
        lambda *refs: owner_in_kernel(task_dev, *refs),
        out_shape=(
            jax.ShapeDtypeStruct((owner_rows, 2 * rank), f32),
            jax.ShapeDtypeStruct((owner_rows, half_width), bf16),
            jax.ShapeDtypeStruct((owner_rows, key_part), bf16),
            jax.ShapeDtypeStruct((owner_rows, 128), bf16),
        ),
        in_specs=[VMEM] * 3,
        out_specs=(VMEM,) * 4,
        compiler_params=PARAMS,
        name="owner_in",
    )(got, down_t, up_t)
    low_other = swap(low_mine, "seq")
    to_return, low_wide, grad_wide = pl.pallas_call(
        lambda *refs: owner_out_kernel(task_dev, *refs),
        out_shape=(
            jax.ShapeDtypeStruct((sent_rows, tw + cw), bf16),
            jax.ShapeDtypeStruct((owner_rows, task_dev * rank), bf16),
            jax.ShapeDtypeStruct((owner_rows, task_dev * rank), bf16),
        ),
        in_specs=[VMEM] * 5,
        out_specs=(VMEM,) * 3,
        scratch_shapes=[
            pltpu.VMEM((owner_rows, half_width), bf16),
            pltpu.VMEM((owner_rows, key_part), bf16),
        ],
        compiler_params=PARAMS,
        name="owner_out",
    )(low_mine, low_other, label_in, down_t, up_t)
    returned = lax.all_to_all(to_return, SUB, split_axis=0, concat_axis=0, tiled=True)

    up_gradient = (adapter_scale * dot(low_wide, cots_in, 0, 0)).reshape(task_dev, rank, key_part)
    down_gradient = (
        dot(grad_wide, rows_in, 0, 0).reshape(task_dev, rank, half_width).transpose(2, 0, 1)
    )

    shard = weight.shape[0]
    held = (SPLIT[0], SPLIT[2], SPLIT[1], shard)
    natural = SPLIT + (shard,)
    other_cot = swap(cotangent, "seq")
    full_cot = jnp.where(
        seq == 0,
        jnp.concatenate([cotangent, other_cot], axis=1),
        jnp.concatenate([other_cot, cotangent], axis=1),
    )
    by_core = full_cot.reshape((rows_dev,) + natural).transpose(0, 4, 1, 3, 2, 5)
    by_core = by_core.reshape(rows_dev, 2, -1)
    cot_first, cot_second = by_core[:, 0], by_core[:, 1]
    own_cot = jnp.where(core == 0, cot_first, cot_second)
    off_cot = jnp.where(core == 0, cot_second, cot_first)
    own_part = dot(tokens, own_weight, 1, 1)
    off_part = dot(tokens, other_weight, 1, 1)
    parts = jnp.where(
        core == 0,
        jnp.stack([own_part, off_part], axis=1),
        jnp.stack([off_part, own_part], axis=1),
    )
    parts = parts.reshape((rows_dev, 2) + held).transpose(0, 2, 4, 3, 1, 5).reshape(rows_dev, -1)
    keep = jnp.where(seq == 0, parts[:, :key_part], parts[:, key_part:])
    give = jnp.where(seq == 0, parts[:, key_part:], parts[:, :key_part])
    frozen = keep + swap(give, "seq")
    base_grad = dot(own_cot, own_weight) + dot(off_cot, other_weight)

    row_key = jnp.repeat(owner_of * chunk, block_rows) + jnp.tile(
        jnp.arange(block_rows, dtype=jnp.int32) * GROUPS, blocks_dev
    )
    grad_tokens, projected = pl.pallas_call(
        finish_kernel,
        out_shape=(
            jax.ShapeDtypeStruct((rows_dev, half_width), bf16),
            jax.ShapeDtypeStruct((rows_dev, key_part), bf16),
        ),
        in_specs=[VMEM] * 5,
        out_specs=(VMEM, VMEM),
        compiler_params=PARAMS,
        name="finish",
    )(row_key[:, None], returned, base_grad, frozen, bias[None, :])
    return (projected, grad_tokens, down_gradient, up_gradient)


def solution(mesh):
    fine = Mesh(mesh.devices.reshape(SPLIT + (mesh.shape["seq"],)), SUB + ("seq",))
    return jax.shard_map(
        on_device,
        mesh=fine,
        in_specs=(
            P(SUB, "seq"),
            P(SUB, "seq"),
            P("seq"),
            P("seq", SUB, None),
            P(SUB, None, "seq"),
            P(SUB, "seq"),
            P(SUB),
            P(),
        ),
        out_specs=(
            P(SUB, "seq"),
            P(SUB, "seq"),
            P("seq", SUB, None),
            P(SUB, None, "seq"),
        ),
        check_vma=False,
    )
```

```python
import jax
import jax.numpy as jnp
from jax import lax
from jax.experimental import pallas as pl
from jax.experimental.pallas import tpu as pltpu
from jax.sharding import Mesh, PartitionSpec as P

adapter_scale = 0.5
GROUPS = 4
SUB = ("y", "xl", "z", "c")
SPLIT = (4, 2, 8, 2)
bf16 = jnp.bfloat16
f32 = jnp.float32
OWNERS = SPLIT[0] * SPLIT[1] * SPLIT[2] * SPLIT[3]
VMEM = pl.BlockSpec(memory_space=pltpu.VMEM)
HBM = pl.BlockSpec(memory_space=pltpu.HBM)
PARAMS = pltpu.CompilerParams(vmem_limit_bytes=40 * 1024 * 1024)
WHOLE = pltpu.CompilerParams(vmem_limit_bytes=60 * 1024 * 1024)


def dot(a, b, da=1, db=0):
    return lax.dot_general(a, b, (((da,), (db,)), ((), ())), preferred_element_type=f32)


def iota(shape, dim):
    return lax.broadcasted_iota(jnp.int32, shape, dim)


def one(condition):
    return jnp.where(condition, 1.0, 0.0).astype(bf16)


def fetch(pairs, sems):
    copies = [pltpu.make_async_copy(a, b, sems.at[i]) for i, (a, b) in enumerate(pairs)]
    for copy in copies:
        copy.start()
    return copies


def pack_kernel(task_ref, slot_ref, tok_ref, cot_ref, out_ref, code_ref, stack, block, sems, out_sems):
    rows, width = tok_ref.shape
    tasks_all = slot_ref.shape[1]
    tw, cw = width // GROUPS, cot_ref.shape[1] // GROUPS
    chunk = out_ref.shape[0] // OWNERS
    task_dev = tasks_all // OWNERS
    pairs = []
    for g in range(GROUPS):
        at = pl.ds(g * rows, rows)
        pairs.append((tok_ref.at[:, pl.ds(g * tw, tw)], stack.at[at, pl.ds(0, tw)]))
        pairs.append((cot_ref.at[:, pl.ds(g * cw, cw)], stack.at[at, pl.ds(tw, cw)]))
    incoming = fetch(pairs, sems)
    slots = slot_ref[...]
    halves = jnp.concatenate([slots // task_dev, slots % task_dev] + [slots * 0] * 6, axis=0)
    blocks = task_ref.shape[1]
    picked = one(iota((tasks_all, blocks), 0) == task_ref[...])
    by_block = dot(halves.astype(f32).astype(bf16), picked).astype(bf16)
    wide = (blocks, GROUPS * rows)
    found = dot(by_block, one(iota(wide, 0) == (iota(wide, 1) % rows) // (rows // blocks)))
    owner = found[0:1, :].astype(jnp.int32)
    stack[:, tw + cw:] = dot(
        (found + 1.0).astype(bf16), one(iota((8, 128), 0) == 1), 0, 0
    ).astype(bf16)
    col = iota((1, GROUPS * rows), 1)
    code = owner * chunk + (col % (chunk // GROUPS)) * GROUPS + col // rows
    code_ref[...] = code
    step = out_ref.shape[0] // 4
    copies = []
    for copy in incoming:
        copy.wait()
    for b in range(4):
        part = slice(b * step, (b + 1) * step)
        hit = one(iota((step, GROUPS * rows), 0) + b * step == code)
        block[part, :tw + cw] = dot(hit, stack[:, :tw + cw]).astype(bf16)
        block[part, tw + cw:] = (dot(hit, stack[:, tw + cw:]) - 1.0).astype(bf16)
        copy = pltpu.make_async_copy(block.at[part], out_ref.at[part], out_sems.at[b])
        copy.start()
        copies.append(copy)
    for copy in copies:
        copy.wait()


def order(chunk, groups):
    out, src = iota((chunk, chunk), 0), iota((chunk, chunk), 1)
    per = chunk // groups
    return one(src == (out % per) * groups + out // per)


def reorder(chunk, groups):
    src, out = iota((chunk, chunk), 1), iota((chunk, chunk), 0)
    per = chunk // groups
    return one(out == (src % per) * groups + src // per)


def collapse(part, label, tasks, rank):
    total = jnp.zeros((part.shape[0], rank), f32)
    for j in range(tasks):
        total = total + jnp.where(label == j, part[:, j * rank:(j + 1) * rank], 0.0)
    return total


def spread(low, label, tasks):
    return jnp.concatenate(
        [jnp.where(label == j, low, 0.0) for j in range(tasks)], axis=1
    ).astype(bf16)


def rows_of(got_ref, rows, cots, label):
    tw, cw = rows.shape[1] // GROUPS, cots.shape[1] // GROUPS
    step = 256
    per = step // GROUPS
    to_rows = order(step, GROUPS)
    for b in range(got_ref.shape[0] // step):
        block = dot(to_rows, got_ref[b * step:(b + 1) * step, :]).astype(bf16)
        at = slice(b * per, (b + 1) * per)
        for g in range(GROUPS):
            piece = block[g * per:(g + 1) * per, :]
            rows[at, g * tw:(g + 1) * tw] = piece[:, :tw]
            cots[at, g * cw:(g + 1) * cw] = piece[:, tw:tw + cw]
        if label is not None:
            label[at, :] = block[:per, tw + cw:]


def owner_in_kernel(tasks, got_ref, down_ref, up_ref, low_ref, label_ref, rows, cots, down, sem):
    rank = down_ref.shape[0] // tasks
    copy = pltpu.make_async_copy(down_ref, down, sem)
    copy.start()
    rows_of(got_ref, rows, cots, label_ref)
    label = label_ref[...].astype(f32)[:, :rank]
    low_ref[:, rank:] = collapse(dot(cots[...], up_ref[...], 1, 1), label, tasks, rank)
    copy.wait()
    low_ref[:, :rank] = collapse(dot(rows[...], down[...], 1, 1), label, tasks, rank)


def wide_lows(tasks, rank, mine_ref, other_ref, label_ref):
    total = mine_ref[...] + other_ref[...]
    label = label_ref[...].astype(f32)[:, :rank]
    low = total[:, :rank].astype(bf16).astype(f32)
    grad = (adapter_scale * total[:, rank:]).astype(bf16).astype(f32)
    return spread(low, label, tasks), spread(grad, label, tasks)


def owner_out_kernel(
    tasks, mine_ref, other_ref, label_ref, down_ref, up_ref, out_ref, back, lora, sent, sems
):
    rank = down_ref.shape[0] // tasks
    width, key_part = down_ref.shape[1], up_ref.shape[1]
    tw, cw = width // GROUPS, key_part // GROUPS
    low_wide, grad_wide = wide_lows(tasks, rank, mine_ref, other_ref, label_ref)
    lora[...] = (adapter_scale * dot(low_wide, up_ref[...])).astype(bf16)
    for g in range(GROUPS):
        cols = slice(g * tw, (g + 1) * tw)
        back[:, cols] = dot(grad_wide, down_ref[:, cols]).astype(bf16)
    step = 256
    per = step // GROUPS
    to_sent = reorder(step, GROUPS)
    copies = []
    for b in range(out_ref.shape[0] // step):
        at = slice(b * per, (b + 1) * per)
        rows = jnp.concatenate([back[at, g * tw:(g + 1) * tw] for g in range(GROUPS)], axis=0)
        adds = jnp.concatenate([lora[at, g * cw:(g + 1) * cw] for g in range(GROUPS)], axis=0)
        part = slice(b * step, (b + 1) * step)
        sent[part, :tw] = dot(to_sent, rows).astype(bf16)
        sent[part, tw:] = dot(to_sent, adds).astype(bf16)
        copy = pltpu.make_async_copy(sent.at[part], out_ref.at[part], sems.at[b])
        copy.start()
        copies.append(copy)
    for copy in copies:
        copy.wait()


def gradients_kernel(
    tasks, got_ref, mine_ref, other_ref, label_ref, down_ref, up_ref, rows, cots
):
    rank = mine_ref.shape[1] // 2
    rows_of(got_ref, rows, cots, None)
    low_wide, grad_wide = wide_lows(tasks, rank, mine_ref, other_ref, label_ref)
    up_ref[...] = adapter_scale * dot(low_wide, cots[...], 0, 0)
    tw = rows.shape[1] // GROUPS
    for g in range(GROUPS):
        cols = slice(g * tw, (g + 1) * tw)
        down_ref[:, cols] = dot(grad_wide, rows[:, cols], 0, 0)


def base_kernel(place_ref, tok_ref, cot_ref, cot2_ref, *rest):
    held, (parts_ref, grad_ref, full, cots, sems) = rest[:-5], rest[-5:]
    y, c, seq = place_ref[0], place_ref[1], place_ref[2]
    width = tok_ref.shape[1]
    near = full.shape[0] // (2 * SPLIT[0])
    shard = near // (SPLIT[1] * SPLIT[2])
    block = 2 * near
    half = SPLIT[0] // 2
    pairs, count = [], len(held) // 2
    for i, ref in enumerate(held):
        rows, columns = ref.shape
        flip, back = i // count, i % count - 1
        if back < 0:
            at, first = 0, 0
        else:
            at, first = lax.rem(y + SPLIT[0] - back, SPLIT[0]), width - columns
        start = pl.multiple_of(flip * SPLIT[0] * near + at * near, near)
        pairs.append((ref, full.at[pl.ds(start, rows), pl.ds(first, columns)]))
    copies = fetch(pairs, sems)
    src, out = iota((near, block), 0), iota((near, block), 1)
    z, xl, k = src // (SPLIT[1] * shard), (src // shard) % SPLIT[1], src % shard
    places = []
    for flip in range(2):
        core = c if flip == 0 else 1 - c
        places.append(one(out == ((xl * SPLIT[2] + z) * SPLIT[3] + core) * shard + k))
    for at in range(SPLIT[0]):
        cols = slice((at % half) * block, (at % half + 1) * block)
        cot = jnp.where(seq == at // half, cot_ref[:, cols], cot2_ref[:, cols])
        for flip in range(2):
            first = (flip * SPLIT[0] + at) * near
            cots[:, first:first + near] = dot(cot, places[flip], 1, 1).astype(bf16)
    for copy in copies:
        copy.wait()
    part = dot(tok_ref[...], full[...], 1, 1)
    high = part.astype(bf16)
    left = part - high.astype(f32)
    mid = left.astype(bf16)
    low = (left - mid.astype(f32)).astype(bf16)
    for at in range(SPLIT[0]):
        moved = 0.0
        for flip in range(2):
            first = (flip * SPLIT[0] + at) * near
            for piece in (high, mid, low):
                moved = moved + dot(piece[:, first:first + near], places[flip])
        cols = slice((at % half) * block, (at % half + 1) * block)
        parts_ref[jnp.where(seq == at // half, 0, 1), :, cols] = moved
    tile = 1024
    for t in range(width // tile):
        cols = slice(t * tile, (t + 1) * tile)
        grad_ref[:, cols] = dot(cots[...], full[:, cols])


def finish_kernel(key_ref, got_ref, base_ref, frozen_ref, bias_ref, grad_ref, proj_ref):
    rows, width = grad_ref.shape
    key_part = proj_ref.shape[1]
    tw, cw = width // GROUPS, key_part // GROUPS
    key = jnp.concatenate([key_ref[...] + g for g in range(GROUPS)], axis=0)
    pick = one(key == iota((GROUPS * rows, got_ref.shape[0]), 1))
    step = 384
    for t in range((tw + cw) // step):
        found = dot(pick, got_ref[:, t * step:(t + 1) * step])
        keep = min(tw - t * step, step)
        for g in range(GROUPS):
            piece = found[g * rows:(g + 1) * rows, :]
            cols = slice(g * tw + t * step, g * tw + t * step + keep)
            grad_ref[:, cols] = (base_ref[:, cols] + piece[:, :keep]).astype(bf16)
            if keep < step:
                keys = slice(g * cw, (g + 1) * cw)
                proj_ref[:, keys] = (
                    frozen_ref[:, keys] + bias_ref[:, keys] + piece[:, keep:]
                ).astype(bf16)


def turn(value, shift):
    n = SPLIT[0]
    return lax.ppermute(value, "y", [(i, (i + shift) % n) for i in range(n)])


def swap(value, axis):
    return lax.ppermute(value, axis, [(0, 1), (1, 0)])


def on_device(tokens, weight, bias, adapter_down, adapter_up, cotangent, block_task, owner_slot):
    rows_dev, half_width = tokens.shape
    owners = OWNERS
    blocks_dev = block_task.shape[0]
    block_rows = rows_dev // blocks_dev
    task_dev, rank, key_part = adapter_up.shape
    chunk = block_rows * GROUPS
    sent_rows = owners * chunk
    tw, cw = half_width // GROUPS, key_part // GROUPS
    seq = lax.axis_index("seq")

    pair = swap(weight, "xl")
    first_x = lax.axis_index("xl") == 0
    pair = jnp.concatenate(
        [jnp.where(first_x, weight, pair), jnp.where(first_x, pair, weight)], axis=0
    )
    tokens_late, pair = lax.optimization_barrier((tokens, pair))
    sent, code = pl.pallas_call(
        pack_kernel,
        out_shape=(
            jax.ShapeDtypeStruct((sent_rows, tw + cw + 128), bf16),
            jax.ShapeDtypeStruct((1, GROUPS * rows_dev), jnp.int32),
        ),
        in_specs=[VMEM, VMEM, HBM, HBM],
        out_specs=(HBM, VMEM),
        scratch_shapes=[
            pltpu.VMEM((GROUPS * rows_dev, tw + cw + 128), bf16),
            pltpu.VMEM((sent_rows, tw + cw + 128), bf16),
            pltpu.SemaphoreType.DMA((2 * GROUPS,)),
            pltpu.SemaphoreType.DMA((4,)),
        ],
        compiler_params=WHOLE,
        name="pack",
    )(block_task[None, :], owner_slot[None, :], tokens_late, cotangent)
    got = lax.all_to_all(sent, SUB, split_axis=0, concat_axis=0, tiled=True)

    slab = lax.all_gather(pair, "z", axis=0, tiled=True)
    cut = half_width // 2
    whole = lax.all_gather(slab[:, :cut], "y", axis=0, tiled=True)
    own = [whole, slab[:, cut:]] + [turn(slab[:, cut:], shift) for shift in range(1, SPLIT[0])]
    weights = own + [swap(part, "c") for part in own]

    down_t = adapter_down.transpose(1, 2, 0).reshape(task_dev * rank, half_width)
    up_t = adapter_up.reshape(task_dev * rank, key_part)
    owner_rows = owners * block_rows
    low_mine, label_in = pl.pallas_call(
        lambda *refs: owner_in_kernel(task_dev, *refs),
        out_shape=(
            jax.ShapeDtypeStruct((owner_rows, 2 * rank), f32),
            jax.ShapeDtypeStruct((owner_rows, 128), bf16),
        ),
        in_specs=[VMEM, HBM, VMEM],
        out_specs=(VMEM,) * 2,
        scratch_shapes=[
            pltpu.VMEM((owner_rows, half_width), bf16),
            pltpu.VMEM((owner_rows, key_part), bf16),
            pltpu.VMEM(down_t.shape, bf16),
            pltpu.SemaphoreType.DMA,
        ],
        compiler_params=PARAMS,
        name="owner_in",
    )(got, down_t, up_t)
    low_other = swap(low_mine, "seq")
    to_return = pl.pallas_call(
        lambda *refs: owner_out_kernel(task_dev, *refs),
        out_shape=jax.ShapeDtypeStruct((sent_rows, tw + cw), bf16),
        in_specs=[VMEM] * 5,
        out_specs=HBM,
        scratch_shapes=[
            pltpu.VMEM((owner_rows, half_width), bf16),
            pltpu.VMEM((owner_rows, key_part), bf16),
            pltpu.VMEM((sent_rows, tw + cw), bf16),
            pltpu.SemaphoreType.DMA((4,)),
        ],
        compiler_params=PARAMS,
        name="owner_out",
    )(low_mine, low_other, label_in, down_t, up_t)
    to_return, _ = lax.optimization_barrier((to_return, own))
    returned = lax.all_to_all(to_return, SUB, split_axis=0, concat_axis=0, tiled=True)

    down_gradient, up_gradient = pl.pallas_call(
        lambda *refs: gradients_kernel(task_dev, *refs),
        out_shape=(
            jax.ShapeDtypeStruct((task_dev * rank, half_width), f32),
            jax.ShapeDtypeStruct((task_dev * rank, key_part), f32),
        ),
        in_specs=[VMEM] * 4,
        out_specs=(VMEM, VMEM),
        scratch_shapes=[
            pltpu.VMEM((owner_rows, half_width), bf16),
            pltpu.VMEM((owner_rows, key_part), bf16),
        ],
        compiler_params=PARAMS,
        name="gradients",
    )(got, low_mine, low_other, label_in)
    up_gradient = up_gradient.reshape(task_dev, rank, key_part)
    down_gradient = down_gradient.reshape(task_dev, rank, half_width).transpose(2, 0, 1)

    other_cot = swap(cotangent, "seq")
    places = jnp.stack([lax.axis_index("y"), lax.axis_index("c"), seq])
    parts, base_grad = pl.pallas_call(
        base_kernel,
        out_shape=(
            jax.ShapeDtypeStruct((2, rows_dev, key_part), f32),
            jax.ShapeDtypeStruct((rows_dev, half_width), f32),
        ),
        in_specs=[pl.BlockSpec(memory_space=pltpu.SMEM)] + [VMEM] * 3 + [HBM] * len(weights),
        out_specs=(VMEM, VMEM),
        scratch_shapes=[
            pltpu.VMEM((2 * key_part, half_width), bf16),
            pltpu.VMEM((rows_dev, 2 * key_part), bf16),
            pltpu.SemaphoreType.DMA((len(weights),)),
        ],
        compiler_params=PARAMS,
        name="base",
    )(places.astype(jnp.int32), tokens, cotangent, other_cot, *weights)
    frozen = parts[0] + swap(parts[1], "seq")

    row_key = code[0, :rows_dev]
    grad_tokens, projected = pl.pallas_call(
        finish_kernel,
        out_shape=(
            jax.ShapeDtypeStruct((rows_dev, half_width), bf16),
            jax.ShapeDtypeStruct((rows_dev, key_part), bf16),
        ),
        in_specs=[VMEM] * 5,
        out_specs=(VMEM, VMEM),
        compiler_params=PARAMS,
        name="finish",
    )(row_key[:, None], returned, base_grad, frozen, bias[None, :])
    return (projected, grad_tokens, down_gradient, up_gradient)


def solution(mesh):
    fine = Mesh(mesh.devices.reshape(SPLIT + (mesh.shape["seq"],)), SUB + ("seq",))
    return jax.shard_map(
        on_device,
        mesh=fine,
        in_specs=(
            P(SUB, "seq"),
            P(SUB, "seq"),
            P("seq"),
            P("seq", SUB, None),
            P(SUB, None, "seq"),
            P(SUB, "seq"),
            P(SUB),
            P(),
        ),
        out_specs=(
            P(SUB, "seq"),
            P(SUB, "seq"),
            P("seq", SUB, None),
            P(SUB, None, "seq"),
        ),
        check_vma=False,
    )
```

```python
import functools

import jax
import jax.numpy as jnp
from jax import lax
from jax.experimental import pallas as pl
from jax.experimental.pallas import tpu as pltpu
from jax.sharding import Mesh, PartitionSpec as P

adapter_scale = 0.5
GROUPS = 4
SUB = ("y", "xl", "z", "c")
SPLIT = (4, 2, 8, 2)
bf16 = jnp.bfloat16
f32 = jnp.float32
OWNERS = SPLIT[0] * SPLIT[1] * SPLIT[2] * SPLIT[3]
VMEM = pl.BlockSpec(memory_space=pltpu.VMEM)
HBM = pl.BlockSpec(memory_space=pltpu.HBM)
PARAMS = pltpu.CompilerParams(vmem_limit_bytes=40 * 1024 * 1024)
WHOLE = pltpu.CompilerParams(vmem_limit_bytes=60 * 1024 * 1024)


def dot(a, b, da=1, db=0):
    return lax.dot_general(a, b, (((da,), (db,)), ((), ())), preferred_element_type=f32)


def iota(shape, dim):
    return lax.broadcasted_iota(jnp.int32, shape, dim)


def one(condition):
    return jnp.where(condition, 1.0, 0.0).astype(bf16)


def fetch(pairs, sems):
    copies = [pltpu.make_async_copy(a, b, sems.at[i]) for i, (a, b) in enumerate(pairs)]
    for copy in copies:
        copy.start()
    return copies


def pack_kernel(task_ref, slot_ref, tok_ref, cot_ref, out_ref, code_ref, stack, block, sems, out_sems):
    rows, width = tok_ref.shape
    tasks_all = slot_ref.shape[1]
    tw, cw = width // GROUPS, cot_ref.shape[1] // GROUPS
    chunk = out_ref.shape[0] // OWNERS
    task_dev = tasks_all // OWNERS
    pairs = []
    for g in range(GROUPS):
        at = pl.ds(g * rows, rows)
        pairs.append((tok_ref.at[:, pl.ds(g * tw, tw)], stack.at[at, pl.ds(0, tw)]))
        pairs.append((cot_ref.at[:, pl.ds(g * cw, cw)], stack.at[at, pl.ds(tw, cw)]))
    incoming = fetch(pairs, sems)
    slots = slot_ref[...]
    halves = jnp.concatenate([slots // task_dev, slots % task_dev] + [slots * 0] * 6, axis=0)
    blocks = task_ref.shape[1]
    picked = one(iota((tasks_all, blocks), 0) == task_ref[...])
    by_block = dot(halves.astype(f32).astype(bf16), picked).astype(bf16)
    wide = (blocks, GROUPS * rows)
    found = dot(by_block, one(iota(wide, 0) == (iota(wide, 1) % rows) // (rows // blocks)))
    owner = found[0:1, :].astype(jnp.int32)
    stack[:, tw + cw:] = dot(
        (found + 1.0).astype(bf16), one(iota((8, 128), 0) == 1), 0, 0
    ).astype(bf16)
    col = iota((1, GROUPS * rows), 1)
    code = owner * chunk + (col % (chunk // GROUPS)) * GROUPS + col // rows
    code_ref[...] = code
    step = out_ref.shape[0] // 4
    copies = []
    for copy in incoming:
        copy.wait()
    for b in range(4):
        part = slice(b * step, (b + 1) * step)
        hit = one(iota((step, GROUPS * rows), 0) + b * step == code)
        block[part, :tw + cw] = dot(hit, stack[:, :tw + cw]).astype(bf16)
        block[part, tw + cw:] = (dot(hit, stack[:, tw + cw:]) - 1.0).astype(bf16)
        copy = pltpu.make_async_copy(block.at[part], out_ref.at[part], out_sems.at[b])
        copy.start()
        copies.append(copy)
    for copy in copies:
        copy.wait()


def order(chunk, groups):
    out, src = iota((chunk, chunk), 0), iota((chunk, chunk), 1)
    per = chunk // groups
    return one(src == (out % per) * groups + out // per)


def reorder(chunk, groups):
    src, out = iota((chunk, chunk), 1), iota((chunk, chunk), 0)
    per = chunk // groups
    return one(out == (src % per) * groups + src // per)


def collapse(part, label, tasks, rank):
    total = jnp.zeros((part.shape[0], rank), f32)
    for j in range(tasks):
        total = total + jnp.where(label == j, part[:, j * rank:(j + 1) * rank], 0.0)
    return total


def spread(low, label, tasks):
    return jnp.concatenate(
        [jnp.where(label == j, low, 0.0) for j in range(tasks)], axis=1
    ).astype(bf16)


def rows_of(got_ref, rows, cots, label):
    tw, cw = rows.shape[1] // GROUPS, cots.shape[1] // GROUPS
    step = 256
    per = step // GROUPS
    to_rows = order(step, GROUPS)
    for b in range(got_ref.shape[0] // step):
        block = dot(to_rows, got_ref[b * step:(b + 1) * step, :]).astype(bf16)
        at = slice(b * per, (b + 1) * per)
        for g in range(GROUPS):
            piece = block[g * per:(g + 1) * per, :]
            rows[at, g * tw:(g + 1) * tw] = piece[:, :tw]
            cots[at, g * cw:(g + 1) * cw] = piece[:, tw:tw + cw]
        if label is not None:
            label[at, :] = block[:per, tw + cw:]


def owner_in_kernel(tasks, got_ref, down_ref, up_ref, low_ref, label_ref, rows, cots, down, sem):
    rank = down_ref.shape[0] // tasks
    copy = pltpu.make_async_copy(down_ref, down, sem)
    copy.start()
    rows_of(got_ref, rows, cots, label_ref)
    label = label_ref[...].astype(f32)[:, :rank]
    low_ref[:, rank:] = collapse(dot(cots[...], up_ref[...], 1, 1), label, tasks, rank)
    copy.wait()
    low_ref[:, :rank] = collapse(dot(rows[...], down[...], 1, 1), label, tasks, rank)


def wide_lows(tasks, rank, mine_ref, other_ref, label_ref):
    total = mine_ref[...] + other_ref[...]
    label = label_ref[...].astype(f32)[:, :rank]
    low = total[:, :rank].astype(bf16).astype(f32)
    grad = (adapter_scale * total[:, rank:]).astype(bf16).astype(f32)
    return spread(low, label, tasks), spread(grad, label, tasks)


def owner_out_kernel(
    tasks, mine_ref, other_ref, label_ref, down_ref, up_ref, out_ref, back, lora, sent, sems
):
    rank = down_ref.shape[0] // tasks
    width, key_part = down_ref.shape[1], up_ref.shape[1]
    tw, cw = width // GROUPS, key_part // GROUPS
    low_wide, grad_wide = wide_lows(tasks, rank, mine_ref, other_ref, label_ref)
    lora[...] = (adapter_scale * dot(low_wide, up_ref[...])).astype(bf16)
    for g in range(GROUPS):
        cols = slice(g * tw, (g + 1) * tw)
        back[:, cols] = dot(grad_wide, down_ref[:, cols]).astype(bf16)
    step = 256
    per = step // GROUPS
    to_sent = reorder(step, GROUPS)
    copies = []
    for b in range(out_ref.shape[0] // step):
        at = slice(b * per, (b + 1) * per)
        rows = jnp.concatenate([back[at, g * tw:(g + 1) * tw] for g in range(GROUPS)], axis=0)
        adds = jnp.concatenate([lora[at, g * cw:(g + 1) * cw] for g in range(GROUPS)], axis=0)
        part = slice(b * step, (b + 1) * step)
        sent[part, :tw] = dot(to_sent, rows).astype(bf16)
        sent[part, tw:] = dot(to_sent, adds).astype(bf16)
        copy = pltpu.make_async_copy(sent.at[part], out_ref.at[part], sems.at[b])
        copy.start()
        copies.append(copy)
    for copy in copies:
        copy.wait()


def gradients_kernel(
    tasks, got_ref, mine_ref, other_ref, label_ref, down_ref, up_ref, rows, cots
):
    rank = mine_ref.shape[1] // 2
    rows_of(got_ref, rows, cots, None)
    low_wide, grad_wide = wide_lows(tasks, rank, mine_ref, other_ref, label_ref)
    up_ref[...] = adapter_scale * dot(low_wide, cots[...], 0, 0)
    tw = rows.shape[1] // GROUPS
    for g in range(GROUPS):
        cols = slice(g * tw, (g + 1) * tw)
        down_ref[:, cols] = dot(grad_wide, rows[:, cols], 0, 0)


def base_kernel(flip, place_ref, tok_ref, cot_ref, cot2_ref, *rest):
    held, rest = rest[:1 + SPLIT[0]], rest[1 + SPLIT[0]:]
    before, (parts_ref, grad_ref, full, cots, sems) = rest[:-5], rest[-5:]
    y, xl, c, seq = (place_ref[i] for i in range(4))
    width = tok_ref.shape[1]
    near = full.shape[0] // SPLIT[0]
    shard = near // (SPLIT[1] * SPLIT[2])
    block = 2 * near
    half = SPLIT[0] // 2
    pairs = []
    for back, ref in enumerate(held, -1):
        rows, columns = ref.shape
        if back < 0:
            at, first = 0, 0
        else:
            at, first = lax.rem(y + SPLIT[0] - back, SPLIT[0]), width - columns
        start = pl.multiple_of(at * near, near)
        pairs.append((ref, full.at[pl.ds(start, rows), pl.ds(first, columns)]))
    copies = fetch(pairs, sems)
    src, out = iota((near, block), 0), iota((near, block), 1)
    xl_of = (src // (SPLIT[2] * shard) + xl) % SPLIT[1]
    z, k = (src // shard) % SPLIT[2], src % shard
    core = c if flip == 0 else 1 - c
    place = one(out == ((xl_of * SPLIT[2] + z) * SPLIT[3] + core) * shard + k)
    for at in range(SPLIT[0]):
        cols = slice((at % half) * block, (at % half + 1) * block)
        cot = jnp.where(seq == at // half, cot_ref[:, cols], cot2_ref[:, cols])
        cots[:, at * near:(at + 1) * near] = dot(cot, place, 1, 1).astype(bf16)
    for copy in copies:
        copy.wait()
    part = dot(tok_ref[...], full[...], 1, 1)
    high = part.astype(bf16)
    left = part - high.astype(f32)
    mid = left.astype(bf16)
    low = (left - mid.astype(f32)).astype(bf16)
    for at in range(SPLIT[0]):
        moved = 0.0
        for piece in (high, mid, low):
            moved = moved + dot(piece[:, at * near:(at + 1) * near], place)
        cols = slice((at % half) * block, (at % half + 1) * block)
        which = jnp.where(seq == at // half, 0, 1)
        if before:
            moved = moved + before[0][which, :, cols]
        parts_ref[which, :, cols] = moved
    tile = 1024
    for t in range(width // tile):
        cols = slice(t * tile, (t + 1) * tile)
        total = dot(cots[...], full[:, cols])
        if before:
            total = total + before[1][:, cols]
        grad_ref[:, cols] = total


def finish_kernel(key_ref, got_ref, base_ref, frozen_ref, bias_ref, grad_ref, proj_ref):
    rows, width = grad_ref.shape
    key_part = proj_ref.shape[1]
    tw, cw = width // GROUPS, key_part // GROUPS
    key = jnp.concatenate([key_ref[...] + g for g in range(GROUPS)], axis=0)
    pick = one(key == iota((GROUPS * rows, got_ref.shape[0]), 1))
    step = 384
    for t in range((tw + cw) // step):
        found = dot(pick, got_ref[:, t * step:(t + 1) * step])
        keep = min(tw - t * step, step)
        for g in range(GROUPS):
            piece = found[g * rows:(g + 1) * rows, :]
            cols = slice(g * tw + t * step, g * tw + t * step + keep)
            grad_ref[:, cols] = (base_ref[:, cols] + piece[:, :keep]).astype(bf16)
            if keep < step:
                keys = slice(g * cw, (g + 1) * cw)
                proj_ref[:, keys] = (
                    frozen_ref[:, keys] + bias_ref[:, keys] + piece[:, keep:]
                ).astype(bf16)


def turn(value, shift):
    n = SPLIT[0]
    return lax.ppermute(value, "y", [(i, (i + shift) % n) for i in range(n)])


def swap(value, axis):
    return lax.ppermute(value, axis, [(0, 1), (1, 0)])


def on_device(tokens, weight, bias, adapter_down, adapter_up, cotangent, block_task, owner_slot):
    rows_dev, half_width = tokens.shape
    owners = OWNERS
    blocks_dev = block_task.shape[0]
    block_rows = rows_dev // blocks_dev
    task_dev, rank, key_part = adapter_up.shape
    chunk = block_rows * GROUPS
    sent_rows = owners * chunk
    tw, cw = half_width // GROUPS, key_part // GROUPS
    seq = lax.axis_index("seq")

    sent, code = pl.pallas_call(
        pack_kernel,
        out_shape=(
            jax.ShapeDtypeStruct((sent_rows, tw + cw + 128), bf16),
            jax.ShapeDtypeStruct((1, GROUPS * rows_dev), jnp.int32),
        ),
        in_specs=[VMEM, VMEM, HBM, HBM],
        out_specs=(HBM, VMEM),
        scratch_shapes=[
            pltpu.VMEM((GROUPS * rows_dev, tw + cw + 128), bf16),
            pltpu.VMEM((sent_rows, tw + cw + 128), bf16),
            pltpu.SemaphoreType.DMA((2 * GROUPS,)),
            pltpu.SemaphoreType.DMA((4,)),
        ],
        compiler_params=WHOLE,
        name="pack",
    )(block_task[None, :], owner_slot[None, :], tokens, cotangent)
    sent, other_cot = lax.optimization_barrier((sent, swap(cotangent, "seq")))
    got = lax.all_to_all(sent, SUB, split_axis=0, concat_axis=0, tiled=True)

    slab = lax.all_gather(weight, ("z", "c"), axis=0).reshape(SPLIT[2], 2, -1, half_width)
    slab = lax.dynamic_index_in_dim(slab, lax.axis_index("c"), 1, keepdims=False)
    slab = slab.reshape(-1, half_width)
    slab = jnp.concatenate([slab, swap(slab, "xl")], axis=0)
    cut = half_width * 3 // 4
    whole = lax.all_gather(slab[:, :cut], "y", axis=0, tiled=True)
    own = [whole, slab[:, cut:]] + [turn(slab[:, cut:], shift) for shift in range(1, SPLIT[0])]

    down_t = adapter_down.transpose(1, 2, 0).reshape(task_dev * rank, half_width)
    up_t = adapter_up.reshape(task_dev * rank, key_part)
    owner_rows = owners * block_rows
    low_mine, label_in = pl.pallas_call(
        lambda *refs: owner_in_kernel(task_dev, *refs),
        out_shape=(
            jax.ShapeDtypeStruct((owner_rows, 2 * rank), f32),
            jax.ShapeDtypeStruct((owner_rows, 128), bf16),
        ),
        in_specs=[VMEM, HBM, VMEM],
        out_specs=(VMEM,) * 2,
        scratch_shapes=[
            pltpu.VMEM((owner_rows, half_width), bf16),
            pltpu.VMEM((owner_rows, key_part), bf16),
            pltpu.VMEM(down_t.shape, bf16),
            pltpu.SemaphoreType.DMA,
        ],
        compiler_params=PARAMS,
        name="owner_in",
    )(got, down_t, up_t)
    low_other = swap(low_mine, "seq")
    to_return = pl.pallas_call(
        lambda *refs: owner_out_kernel(task_dev, *refs),
        out_shape=jax.ShapeDtypeStruct((sent_rows, tw + cw), bf16),
        in_specs=[VMEM] * 5,
        out_specs=HBM,
        scratch_shapes=[
            pltpu.VMEM((owner_rows, half_width), bf16),
            pltpu.VMEM((owner_rows, key_part), bf16),
            pltpu.VMEM((sent_rows, tw + cw), bf16),
            pltpu.SemaphoreType.DMA((4,)),
        ],
        compiler_params=PARAMS,
        name="owner_out",
    )(low_mine, low_other, label_in, down_t, up_t)
    to_return, _ = lax.optimization_barrier((to_return, own[1:]))
    returned = lax.all_to_all(to_return, SUB, split_axis=0, concat_axis=0, tiled=True)

    down_gradient, up_gradient = pl.pallas_call(
        lambda *refs: gradients_kernel(task_dev, *refs),
        out_shape=(
            jax.ShapeDtypeStruct((task_dev * rank, half_width), f32),
            jax.ShapeDtypeStruct((task_dev * rank, key_part), f32),
        ),
        in_specs=[VMEM] * 4,
        out_specs=(VMEM, VMEM),
        scratch_shapes=[
            pltpu.VMEM((owner_rows, half_width), bf16),
            pltpu.VMEM((owner_rows, key_part), bf16),
        ],
        compiler_params=PARAMS,
        name="gradients",
    )(got, low_mine, low_other, label_in)
    up_gradient = up_gradient.reshape(task_dev, rank, key_part)
    down_gradient = down_gradient.reshape(task_dev, rank, half_width).transpose(2, 0, 1)

    places = jnp.stack([lax.axis_index("y"), lax.axis_index("xl"), lax.axis_index("c"), seq])
    before = ()
    for flip, held in enumerate((own, [swap(part, "c") for part in own])):
        before = pl.pallas_call(
            functools.partial(base_kernel, flip),
            out_shape=(
                jax.ShapeDtypeStruct((2, rows_dev, key_part), f32),
                jax.ShapeDtypeStruct((rows_dev, half_width), f32),
            ),
            in_specs=[pl.BlockSpec(memory_space=pltpu.SMEM)]
            + [VMEM] * 3 + [HBM] * len(held) + [VMEM] * len(before),
            out_specs=(VMEM, VMEM),
            scratch_shapes=[
                pltpu.VMEM((key_part, half_width), bf16),
                pltpu.VMEM((rows_dev, key_part), bf16),
                pltpu.SemaphoreType.DMA((len(held),)),
            ],
            compiler_params=PARAMS,
            name=("base_own", "base_other")[flip],
        )(places.astype(jnp.int32), tokens, cotangent, other_cot, *held, *before)
    parts, base_grad = before
    frozen = parts[0] + swap(parts[1], "seq")

    row_key = code[0, :rows_dev]
    grad_tokens, projected = pl.pallas_call(
        finish_kernel,
        out_shape=(
            jax.ShapeDtypeStruct((rows_dev, half_width), bf16),
            jax.ShapeDtypeStruct((rows_dev, key_part), bf16),
        ),
        in_specs=[VMEM] * 5,
        out_specs=(VMEM, VMEM),
        compiler_params=PARAMS,
        name="finish",
    )(row_key[:, None], returned, base_grad, frozen, bias[None, :])
    return (projected, grad_tokens, down_gradient, up_gradient)


def solution(mesh):
    fine = Mesh(mesh.devices.reshape(SPLIT + (mesh.shape["seq"],)), SUB + ("seq",))
    return jax.shard_map(
        on_device,
        mesh=fine,
        in_specs=(
            P(SUB, "seq"),
            P(SUB, "seq"),
            P("seq"),
            P("seq", SUB, None),
            P(SUB, None, "seq"),
            P(SUB, "seq"),
            P(SUB),
            P(),
        ),
        out_specs=(
            P(SUB, "seq"),
            P(SUB, "seq"),
            P("seq", SUB, None),
            P(SUB, None, "seq"),
        ),
        check_vma=False,
    )
```

```python
import functools

import jax
import jax.numpy as jnp
from jax import lax
from jax.experimental import pallas as pl
from jax.experimental.pallas import tpu as pltpu
from jax.sharding import Mesh, PartitionSpec as P

adapter_scale = 0.5
GROUPS = 4
SUB = ("y", "xl", "z", "c")
SPLIT = (4, 2, 8, 2)
bf16 = jnp.bfloat16
f32 = jnp.float32
OWNERS = SPLIT[0] * SPLIT[1] * SPLIT[2] * SPLIT[3]
VMEM = pl.BlockSpec(memory_space=pltpu.VMEM)
HBM = pl.BlockSpec(memory_space=pltpu.HBM)
PARAMS = pltpu.CompilerParams(vmem_limit_bytes=20 * 1024 * 1024)
WHOLE = pltpu.CompilerParams(vmem_limit_bytes=60 * 1024 * 1024)


def dot(a, b, da=1, db=0):
    return lax.dot_general(a, b, (((da,), (db,)), ((), ())), preferred_element_type=f32)


def iota(shape, dim):
    return lax.broadcasted_iota(jnp.int32, shape, dim)


def one(condition):
    return jnp.where(condition, 1.0, 0.0).astype(bf16)


def fetch(pairs, sems):
    copies = [pltpu.make_async_copy(a, b, sems.at[i]) for i, (a, b) in enumerate(pairs)]
    for copy in copies:
        copy.start()
    return copies


def pack_kernel(task_ref, slot_ref, tok_ref, cot_ref, out_ref, code_ref, stack, block, out_sems):
    rows, width = tok_ref.shape
    tasks_all = slot_ref.shape[1]
    tw, cw = width // GROUPS, cot_ref.shape[1] // GROUPS
    chunk = out_ref.shape[0] // OWNERS
    task_dev = tasks_all // OWNERS
    for g in range(GROUPS):
        at = slice(g * rows, (g + 1) * rows)
        stack[at, :tw] = tok_ref[:, g * tw:(g + 1) * tw]
        stack[at, tw:tw + cw] = cot_ref[:, g * cw:(g + 1) * cw]
    slots = slot_ref[...]
    halves = jnp.concatenate([slots // task_dev, slots % task_dev] + [slots * 0] * 6, axis=0)
    blocks = task_ref.shape[1]
    picked = one(iota((tasks_all, blocks), 0) == task_ref[...])
    by_block = dot(halves.astype(f32).astype(bf16), picked).astype(bf16)
    wide = (blocks, GROUPS * rows)
    found = dot(by_block, one(iota(wide, 0) == (iota(wide, 1) % rows) // (rows // blocks)))
    owner = found[0:1, :].astype(jnp.int32)
    stack[:, tw + cw:] = dot(
        (found + 1.0).astype(bf16), one(iota((8, 128), 0) == 1), 0, 0
    ).astype(bf16)
    col = iota((1, GROUPS * rows), 1)
    code = owner * chunk + (col % (chunk // GROUPS)) * GROUPS + col // rows
    code_ref[...] = code
    step = out_ref.shape[0] // 4
    copies = []
    for b in range(4):
        part = slice(b * step, (b + 1) * step)
        hit = one(iota((step, GROUPS * rows), 0) + b * step == code)
        block[part, :tw + cw] = dot(hit, stack[:, :tw + cw]).astype(bf16)
        block[part, tw + cw:] = (dot(hit, stack[:, tw + cw:]) - 1.0).astype(bf16)
        copy = pltpu.make_async_copy(block.at[part], out_ref.at[part], out_sems.at[b])
        copy.start()
        copies.append(copy)
    for copy in copies:
        copy.wait()


def order(chunk, groups):
    out, src = iota((chunk, chunk), 0), iota((chunk, chunk), 1)
    per = chunk // groups
    return one(src == (out % per) * groups + out // per)


def reorder(chunk, groups):
    src, out = iota((chunk, chunk), 1), iota((chunk, chunk), 0)
    per = chunk // groups
    return one(out == (src % per) * groups + src // per)


def collapse(part, label, tasks, rank):
    total = jnp.zeros((part.shape[0], rank), f32)
    for j in range(tasks):
        total = total + jnp.where(label == j, part[:, j * rank:(j + 1) * rank], 0.0)
    return total


def spread(low, label, tasks):
    return jnp.concatenate(
        [jnp.where(label == j, low, 0.0) for j in range(tasks)], axis=1
    ).astype(bf16)


def rows_of(got_ref, rows, cots, label):
    tw, cw = rows.shape[1] // GROUPS, cots.shape[1] // GROUPS
    step = 256
    per = step // GROUPS
    to_rows = order(step, GROUPS)
    for b in range(got_ref.shape[0] // step):
        block = dot(to_rows, got_ref[b * step:(b + 1) * step, :]).astype(bf16)
        at = slice(b * per, (b + 1) * per)
        for g in range(GROUPS):
            piece = block[g * per:(g + 1) * per, :]
            rows[at, g * tw:(g + 1) * tw] = piece[:, :tw]
            cots[at, g * cw:(g + 1) * cw] = piece[:, tw:tw + cw]
        if label is not None:
            label[at, :] = block[:per, tw + cw:]


def rows_kernel(got_ref, rows_ref, cots_ref, label_ref):
    rows_of(got_ref, rows_ref, cots_ref, label_ref)


def low_kernel(tasks, rows_ref, cots_ref, label_ref, down_ref, up_ref, low_ref):
    rank = down_ref.shape[0] // tasks
    label = label_ref[...].astype(f32)[:, :rank]
    low_ref[:, rank:] = collapse(dot(cots_ref[...], up_ref[...], 1, 1), label, tasks, rank)
    low_ref[:, :rank] = collapse(dot(rows_ref[...], down_ref[...], 1, 1), label, tasks, rank)


def wide_lows(tasks, rank, mine_ref, other_ref, label_ref):
    total = mine_ref[...] + other_ref[...]
    label = label_ref[...].astype(f32)[:, :rank]
    low = total[:, :rank].astype(bf16).astype(f32)
    grad = (adapter_scale * total[:, rank:]).astype(bf16).astype(f32)
    return spread(low, label, tasks), spread(grad, label, tasks)


def owner_out_kernel(
    tasks, mine_ref, other_ref, label_ref, down_ref, up_ref, out_ref, back, lora, sent, sems
):
    rank = down_ref.shape[0] // tasks
    width, key_part = down_ref.shape[1], up_ref.shape[1]
    tw, cw = width // GROUPS, key_part // GROUPS
    low_wide, grad_wide = wide_lows(tasks, rank, mine_ref, other_ref, label_ref)
    lora[...] = (adapter_scale * dot(low_wide, up_ref[...])).astype(bf16)
    for g in range(GROUPS):
        cols = slice(g * tw, (g + 1) * tw)
        back[:, cols] = dot(grad_wide, down_ref[:, cols]).astype(bf16)
    step = 256
    per = step // GROUPS
    to_sent = reorder(step, GROUPS)
    copies = []
    for b in range(out_ref.shape[0] // step):
        at = slice(b * per, (b + 1) * per)
        rows = jnp.concatenate([back[at, g * tw:(g + 1) * tw] for g in range(GROUPS)], axis=0)
        adds = jnp.concatenate([lora[at, g * cw:(g + 1) * cw] for g in range(GROUPS)], axis=0)
        part = slice(b * step, (b + 1) * step)
        sent[part, :tw] = dot(to_sent, rows).astype(bf16)
        sent[part, tw:] = dot(to_sent, adds).astype(bf16)
        copy = pltpu.make_async_copy(sent.at[part], out_ref.at[part], sems.at[b])
        copy.start()
        copies.append(copy)
    for copy in copies:
        copy.wait()


def gradients_kernel(
    tasks, got_ref, mine_ref, other_ref, label_ref, down_ref, up_ref, rows, cots
):
    rank = mine_ref.shape[1] // 2
    rows_of(got_ref, rows, cots, None)
    low_wide, grad_wide = wide_lows(tasks, rank, mine_ref, other_ref, label_ref)
    up_ref[...] = adapter_scale * dot(low_wide, cots[...], 0, 0)
    tw = rows.shape[1] // GROUPS
    for g in range(GROUPS):
        cols = slice(g * tw, (g + 1) * tw)
        down_ref[:, cols] = dot(grad_wide, rows[:, cols], 0, 0)


def base_kernel(flip, place_ref, tok_ref, cot_ref, cot2_ref, *rest):
    held, rest = rest[:1 + SPLIT[0]], rest[1 + SPLIT[0]:]
    before, (parts_ref, grad_ref, full, cots, sems) = rest[:-5], rest[-5:]
    y, xl, c, seq = (place_ref[i] for i in range(4))
    width = tok_ref.shape[1]
    near = full.shape[0] // SPLIT[0]
    shard = near // (SPLIT[1] * SPLIT[2])
    block = 2 * near
    half = SPLIT[0] // 2
    pairs = []
    for back, ref in enumerate(held, -1):
        rows, columns = ref.shape
        if back < 0:
            at, first = 0, 0
        else:
            at, first = lax.rem(y + SPLIT[0] - back, SPLIT[0]), width - columns
        start = pl.multiple_of(at * near, near)
        pairs.append((ref, full.at[pl.ds(start, rows), pl.ds(first, columns)]))
    copies = fetch(pairs, sems)
    src, out = iota((near, block), 0), iota((near, block), 1)
    xl_of = (src // (SPLIT[2] * shard) + xl) % SPLIT[1]
    z, k = (src // shard) % SPLIT[2], src % shard
    core = c if flip == 0 else 1 - c
    place = one(out == ((xl_of * SPLIT[2] + z) * SPLIT[3] + core) * shard + k)
    for at in range(SPLIT[0]):
        cols = slice((at % half) * block, (at % half + 1) * block)
        cot = jnp.where(seq == at // half, cot_ref[:, cols], cot2_ref[:, cols])
        cots[:, at * near:(at + 1) * near] = dot(cot, place, 1, 1).astype(bf16)
    for copy in copies:
        copy.wait()
    part = dot(tok_ref[...], full[...], 1, 1)
    high = part.astype(bf16)
    left = part - high.astype(f32)
    mid = left.astype(bf16)
    low = (left - mid.astype(f32)).astype(bf16)
    for at in range(SPLIT[0]):
        moved = 0.0
        for piece in (high, mid, low):
            moved = moved + dot(piece[:, at * near:(at + 1) * near], place)
        cols = slice((at % half) * block, (at % half + 1) * block)
        which = jnp.where(seq == at // half, 0, 1)
        if before:
            moved = moved + before[0][which, :, cols]
        parts_ref[which, :, cols] = moved
    tile = 1024
    for t in range(width // tile):
        cols = slice(t * tile, (t + 1) * tile)
        total = dot(cots[...], full[:, cols])
        if before:
            total = total + before[1][:, cols]
        grad_ref[:, cols] = total


def pick_kernel(key_ref, got_ref, found_ref):
    rows = key_ref.shape[0]
    key = jnp.concatenate([key_ref[...] + g for g in range(GROUPS)], axis=0)
    pick = one(key == iota((GROUPS * rows, got_ref.shape[0]), 1))
    step = 384
    for t in range(found_ref.shape[1] // step):
        cols = slice(t * step, (t + 1) * step)
        found_ref[:, cols] = dot(pick, got_ref[:, cols])


def finish_kernel(found_ref, base_ref, frozen_ref, bias_ref, grad_ref, proj_ref):
    tw = grad_ref.shape[1]
    grad_ref[...] = (base_ref[...] + found_ref[:, :tw]).astype(bf16)
    proj_ref[...] = (frozen_ref[...] + bias_ref[...] + found_ref[:, tw:]).astype(bf16)


def turn(value, shift):
    n = SPLIT[0]
    return lax.ppermute(value, "y", [(i, (i + shift) % n) for i in range(n)])


def swap(value, axis):
    return lax.ppermute(value, axis, [(0, 1), (1, 0)])


def on_device(tokens, weight, bias, adapter_down, adapter_up, cotangent, block_task, owner_slot):
    rows_dev, half_width = tokens.shape
    owners = OWNERS
    blocks_dev = block_task.shape[0]
    block_rows = rows_dev // blocks_dev
    task_dev, rank, key_part = adapter_up.shape
    chunk = block_rows * GROUPS
    sent_rows = owners * chunk
    tw, cw = half_width // GROUPS, key_part // GROUPS
    seq = lax.axis_index("seq")

    sent, code = pl.pallas_call(
        pack_kernel,
        out_shape=(
            jax.ShapeDtypeStruct((sent_rows, tw + cw + 128), bf16),
            jax.ShapeDtypeStruct((1, GROUPS * rows_dev), jnp.int32),
        ),
        in_specs=[VMEM] * 4,
        out_specs=(HBM, VMEM),
        scratch_shapes=[
            pltpu.VMEM((GROUPS * rows_dev, tw + cw + 128), bf16),
            pltpu.VMEM((sent_rows, tw + cw + 128), bf16),
            pltpu.SemaphoreType.DMA((4,)),
        ],
        compiler_params=WHOLE,
        name="pack",
    )(block_task[None, :], owner_slot[None, :], tokens, cotangent)
    other_cot = swap(cotangent, "seq")
    got = lax.all_to_all(sent, SUB, split_axis=0, concat_axis=0, tiled=True)

    slab = lax.all_gather(weight, ("z", "c"), axis=0).reshape(SPLIT[2], 2, -1, half_width)
    slab = lax.dynamic_index_in_dim(slab, lax.axis_index("c"), 1, keepdims=False)
    slab = slab.reshape(-1, half_width)
    slab = jnp.concatenate([slab, swap(slab, "xl")], axis=0)
    cut = half_width * 3 // 4
    whole = lax.all_gather(slab[:, :cut], "y", axis=0, tiled=True)
    own = [whole, slab[:, cut:]] + [turn(slab[:, cut:], shift) for shift in range(1, SPLIT[0])]

    down_t = adapter_down.transpose(1, 2, 0).reshape(task_dev * rank, half_width)
    up_t = adapter_up.reshape(task_dev * rank, key_part)
    owner_rows = owners * block_rows
    rows_in, cots_in, label_in = pl.pallas_call(
        rows_kernel,
        out_shape=(
            jax.ShapeDtypeStruct((owner_rows, half_width), bf16),
            jax.ShapeDtypeStruct((owner_rows, key_part), bf16),
            jax.ShapeDtypeStruct((owner_rows, 128), bf16),
        ),
        in_specs=[VMEM],
        out_specs=(VMEM,) * 3,
        compiler_params=PARAMS,
        name="owner_rows",
    )(got)
    low_mine = pl.pallas_call(
        functools.partial(low_kernel, task_dev),
        out_shape=jax.ShapeDtypeStruct((owner_rows, 2 * rank), f32),
        in_specs=[VMEM] * 5,
        out_specs=VMEM,
        compiler_params=PARAMS,
        name="owner_in",
    )(rows_in, cots_in, label_in, down_t, up_t)
    low_other = swap(low_mine, "seq")
    to_return = pl.pallas_call(
        lambda *refs: owner_out_kernel(task_dev, *refs),
        out_shape=jax.ShapeDtypeStruct((sent_rows, tw + cw), bf16),
        in_specs=[VMEM] * 5,
        out_specs=HBM,
        scratch_shapes=[
            pltpu.VMEM((owner_rows, half_width), bf16),
            pltpu.VMEM((owner_rows, key_part), bf16),
            pltpu.VMEM((sent_rows, tw + cw), bf16),
            pltpu.SemaphoreType.DMA((4,)),
        ],
        compiler_params=pltpu.CompilerParams(vmem_limit_bytes=50 * 1024 * 1024),
        name="owner_out",
    )(low_mine, low_other, label_in, down_t, up_t)
    to_return, _ = lax.optimization_barrier((to_return, own[1:]))
    returned = lax.all_to_all(to_return, SUB, split_axis=0, concat_axis=0, tiled=True)

    down_gradient, up_gradient = pl.pallas_call(
        lambda *refs: gradients_kernel(task_dev, *refs),
        out_shape=(
            jax.ShapeDtypeStruct((task_dev * rank, half_width), f32),
            jax.ShapeDtypeStruct((task_dev * rank, key_part), f32),
        ),
        in_specs=[VMEM] * 4,
        out_specs=(VMEM, VMEM),
        scratch_shapes=[
            pltpu.VMEM((owner_rows, half_width), bf16),
            pltpu.VMEM((owner_rows, key_part), bf16),
        ],
        compiler_params=PARAMS,
        name="gradients",
    )(got, low_mine, low_other, label_in)
    up_gradient = up_gradient.reshape(task_dev, rank, key_part)
    down_gradient = down_gradient.reshape(task_dev, rank, half_width).transpose(2, 0, 1)

    places = jnp.stack([lax.axis_index("y"), lax.axis_index("xl"), lax.axis_index("c"), seq])
    before = ()
    for flip, held in enumerate((own, [swap(part, "c") for part in own])):
        before = pl.pallas_call(
            functools.partial(base_kernel, flip),
            out_shape=(
                jax.ShapeDtypeStruct((2, rows_dev, key_part), f32),
                jax.ShapeDtypeStruct((rows_dev, half_width), f32),
            ),
            in_specs=[pl.BlockSpec(memory_space=pltpu.SMEM)]
            + [VMEM] * 3 + [HBM] * len(held) + [VMEM] * len(before),
            out_specs=(VMEM, VMEM),
            scratch_shapes=[
                pltpu.VMEM((key_part, half_width), bf16),
                pltpu.VMEM((rows_dev, key_part), bf16),
                pltpu.SemaphoreType.DMA((len(held),)),
            ],
            compiler_params=PARAMS,
            name=("base_own", "base_other")[flip],
        )(places.astype(jnp.int32), tokens, cotangent, other_cot, *held, *before)
    parts, base_grad = before
    frozen = parts[0] + swap(parts[1], "seq")

    row_key = code[0, :rows_dev]
    found = pl.pallas_call(
        pick_kernel,
        out_shape=jax.ShapeDtypeStruct((GROUPS * rows_dev, tw + cw), f32),
        in_specs=[VMEM, VMEM],
        out_specs=VMEM,
        compiler_params=PARAMS,
        name="pick",
    )(row_key[:, None], returned)
    grad_tokens, projected = pl.pallas_call(
        finish_kernel,
        out_shape=(
            jax.ShapeDtypeStruct((rows_dev, half_width), bf16),
            jax.ShapeDtypeStruct((rows_dev, key_part), bf16),
        ),
        grid=(GROUPS,),
        in_specs=[
            pl.BlockSpec((rows_dev, tw + cw), lambda g: (g, 0)),
            pl.BlockSpec((rows_dev, tw), lambda g: (0, g)),
            pl.BlockSpec((rows_dev, cw), lambda g: (0, g)),
            pl.BlockSpec((1, cw), lambda g: (0, g)),
        ],
        out_specs=(
            pl.BlockSpec((rows_dev, tw), lambda g: (0, g)),
            pl.BlockSpec((rows_dev, cw), lambda g: (0, g)),
        ),
        compiler_params=PARAMS,
        name="finish",
    )(found, base_grad, frozen, bias[None, :])
    return (projected, grad_tokens, down_gradient, up_gradient)


def solution(mesh):
    fine = Mesh(mesh.devices.reshape(SPLIT + (mesh.shape["seq"],)), SUB + ("seq",))
    return jax.shard_map(
        on_device,
        mesh=fine,
        in_specs=(
            P(SUB, "seq"),
            P(SUB, "seq"),
            P("seq"),
            P("seq", SUB, None),
            P(SUB, None, "seq"),
            P(SUB, "seq"),
            P(SUB),
            P(),
        ),
        out_specs=(
            P(SUB, "seq"),
            P(SUB, "seq"),
            P("seq", SUB, None),
            P(SUB, None, "seq"),
        ),
        check_vma=False,
    )
```

```python
import functools

import jax
import jax.numpy as jnp
from jax import lax
from jax.experimental import pallas as pl
from jax.experimental.pallas import tpu as pltpu
from jax.sharding import Mesh, PartitionSpec as P

adapter_scale = 0.5
GROUPS = 4
SUB = ("y", "xl", "z", "c")
SPLIT = (4, 2, 8, 2)
bf16 = jnp.bfloat16
f32 = jnp.float32
OWNERS = SPLIT[0] * SPLIT[1] * SPLIT[2] * SPLIT[3]
VMEM = pl.BlockSpec(memory_space=pltpu.VMEM)
HBM = pl.BlockSpec(memory_space=pltpu.HBM)
PARAMS = pltpu.CompilerParams(vmem_limit_bytes=20 * 1024 * 1024)
WHOLE = pltpu.CompilerParams(vmem_limit_bytes=60 * 1024 * 1024)


def dot(a, b, da=1, db=0):
    return lax.dot_general(a, b, (((da,), (db,)), ((), ())), preferred_element_type=f32)


def iota(shape, dim):
    return lax.broadcasted_iota(jnp.int32, shape, dim)


def one(condition):
    return jnp.where(condition, 1.0, 0.0).astype(bf16)


def fetch(pairs, sems):
    copies = [pltpu.make_async_copy(a, b, sems.at[i]) for i, (a, b) in enumerate(pairs)]
    for copy in copies:
        copy.start()
    return copies


def pack_kernel(task_ref, slot_ref, tok_ref, cot_ref, out_ref, code_ref, stack, block, out_sems):
    rows, width = tok_ref.shape
    tasks_all = slot_ref.shape[1]
    tw, cw = width // GROUPS, cot_ref.shape[1] // GROUPS
    chunk = out_ref.shape[0] // OWNERS
    task_dev = tasks_all // OWNERS
    for g in range(GROUPS):
        at = slice(g * rows, (g + 1) * rows)
        stack[at, :tw] = tok_ref[:, g * tw:(g + 1) * tw]
        stack[at, tw:tw + cw] = cot_ref[:, g * cw:(g + 1) * cw]
    slots = slot_ref[...]
    halves = jnp.concatenate([slots // task_dev, slots % task_dev] + [slots * 0] * 6, axis=0)
    blocks = task_ref.shape[1]
    picked = one(iota((tasks_all, blocks), 0) == task_ref[...])
    by_block = dot(halves.astype(f32).astype(bf16), picked).astype(bf16)
    wide = (blocks, GROUPS * rows)
    found = dot(by_block, one(iota(wide, 0) == (iota(wide, 1) % rows) // (rows // blocks)))
    owner = found[0:1, :].astype(jnp.int32)
    stack[:, tw + cw:] = dot(
        (found + 1.0).astype(bf16), one(iota((8, 128), 0) == 1), 0, 0
    ).astype(bf16)
    col = iota((1, GROUPS * rows), 1)
    code = owner * chunk + (col % (chunk // GROUPS)) * GROUPS + col // rows
    code_ref[...] = code
    step = out_ref.shape[0] // 4
    copies = []
    for b in range(4):
        part = slice(b * step, (b + 1) * step)
        hit = one(iota((step, GROUPS * rows), 0) + b * step == code)
        block[part, :tw + cw] = dot(hit, stack[:, :tw + cw]).astype(bf16)
        block[part, tw + cw:] = (dot(hit, stack[:, tw + cw:]) - 1.0).astype(bf16)
        copy = pltpu.make_async_copy(block.at[part], out_ref.at[part], out_sems.at[b])
        copy.start()
        copies.append(copy)
    for copy in copies:
        copy.wait()


def order(chunk, groups):
    out, src = iota((chunk, chunk), 0), iota((chunk, chunk), 1)
    per = chunk // groups
    return one(src == (out % per) * groups + out // per)


def reorder(chunk, groups):
    src, out = iota((chunk, chunk), 1), iota((chunk, chunk), 0)
    per = chunk // groups
    return one(out == (src % per) * groups + src // per)


def collapse(part, label, tasks, rank):
    total = jnp.zeros((part.shape[0], rank), f32)
    for j in range(tasks):
        total = total + jnp.where(label == j, part[:, j * rank:(j + 1) * rank], 0.0)
    return total


def spread(low, label, tasks):
    return jnp.concatenate(
        [jnp.where(label == j, low, 0.0) for j in range(tasks)], axis=1
    ).astype(bf16)


def rows_of(got_ref, rows, cots, label):
    tw, cw = rows.shape[1] // GROUPS, cots.shape[1] // GROUPS
    step = 256
    per = step // GROUPS
    to_rows = order(step, GROUPS)
    for b in range(got_ref.shape[0] // step):
        block = dot(to_rows, got_ref[b * step:(b + 1) * step, :]).astype(bf16)
        at = slice(b * per, (b + 1) * per)
        for g in range(GROUPS):
            piece = block[g * per:(g + 1) * per, :]
            rows[at, g * tw:(g + 1) * tw] = piece[:, :tw]
            cots[at, g * cw:(g + 1) * cw] = piece[:, tw:tw + cw]
        if label is not None:
            label[at, :] = block[:per, tw + cw:]


def rows_kernel(got_ref, rows_ref, cots_ref, label_ref):
    rows_of(got_ref, rows_ref, cots_ref, label_ref)


def low_kernel(tasks, rows_ref, cots_ref, label_ref, down_ref, up_ref, low_ref):
    rank = down_ref.shape[0] // tasks
    label = label_ref[...].astype(f32)[:, :rank]
    low_ref[:, rank:] = collapse(dot(cots_ref[...], up_ref[...], 1, 1), label, tasks, rank)
    low_ref[:, :rank] = collapse(dot(rows_ref[...], down_ref[...], 1, 1), label, tasks, rank)


def wide_lows(tasks, rank, mine_ref, other_ref, label_ref):
    total = mine_ref[...] + other_ref[...]
    label = label_ref[...].astype(f32)[:, :rank]
    low = total[:, :rank].astype(bf16).astype(f32)
    grad = (adapter_scale * total[:, rank:]).astype(bf16).astype(f32)
    return spread(low, label, tasks), spread(grad, label, tasks)


def owner_out_kernel(
    tasks, mine_ref, other_ref, label_ref, down_ref, up_ref, out_ref, back, lora, sent, sems
):
    rank = down_ref.shape[0] // tasks
    width, key_part = down_ref.shape[1], up_ref.shape[1]
    tw, cw = width // GROUPS, key_part // GROUPS
    low_wide, grad_wide = wide_lows(tasks, rank, mine_ref, other_ref, label_ref)
    lora[...] = (adapter_scale * dot(low_wide, up_ref[...])).astype(bf16)
    for g in range(GROUPS):
        cols = slice(g * tw, (g + 1) * tw)
        back[:, cols] = dot(grad_wide, down_ref[:, cols]).astype(bf16)
    step = 256
    per = step // GROUPS
    to_sent = reorder(step, GROUPS)
    copies = []
    for b in range(out_ref.shape[0] // step):
        at = slice(b * per, (b + 1) * per)
        rows = jnp.concatenate([back[at, g * tw:(g + 1) * tw] for g in range(GROUPS)], axis=0)
        adds = jnp.concatenate([lora[at, g * cw:(g + 1) * cw] for g in range(GROUPS)], axis=0)
        part = slice(b * step, (b + 1) * step)
        sent[part, :tw] = dot(to_sent, rows).astype(bf16)
        sent[part, tw:] = dot(to_sent, adds).astype(bf16)
        copy = pltpu.make_async_copy(sent.at[part], out_ref.at[part], sems.at[b])
        copy.start()
        copies.append(copy)
    for copy in copies:
        copy.wait()


def gradients_kernel(
    tasks, got_ref, mine_ref, other_ref, label_ref, down_ref, up_ref, rows, cots
):
    rank = mine_ref.shape[1] // 2
    rows_of(got_ref, rows, cots, None)
    low_wide, grad_wide = wide_lows(tasks, rank, mine_ref, other_ref, label_ref)
    up_ref[...] = adapter_scale * dot(low_wide, cots[...], 0, 0)
    tw = rows.shape[1] // GROUPS
    for g in range(GROUPS):
        cols = slice(g * tw, (g + 1) * tw)
        down_ref[:, cols] = dot(grad_wide, rows[:, cols], 0, 0)


def base_kernel(flip, place_ref, tok_ref, cot_ref, cot2_ref, *rest):
    held, rest = rest[:1 + SPLIT[0]], rest[1 + SPLIT[0]:]
    before, (parts_ref, grad_ref, full, cots, sems) = rest[:-5], rest[-5:]
    y, xl, c, seq = (place_ref[i] for i in range(4))
    width = tok_ref.shape[1]
    near = full.shape[0] // SPLIT[0]
    shard = near // (SPLIT[1] * SPLIT[2])
    block = 2 * near
    half = SPLIT[0] // 2
    pairs = []
    for back, ref in enumerate(held, -1):
        rows, columns = ref.shape
        if back < 0:
            at, first = 0, 0
        else:
            at, first = lax.rem(y + SPLIT[0] - back, SPLIT[0]), width - columns
        start = pl.multiple_of(at * near, near)
        pairs.append((ref, full.at[pl.ds(start, rows), pl.ds(first, columns)]))
    copies = fetch(pairs, sems)
    src, out = iota((near, block), 0), iota((near, block), 1)
    xl_of = (src // (SPLIT[2] * shard) + xl) % SPLIT[1]
    z, k = (src // shard) % SPLIT[2], src % shard
    core = c if flip == 0 else 1 - c
    place = one(out == ((xl_of * SPLIT[2] + z) * SPLIT[3] + core) * shard + k)
    for at in range(SPLIT[0]):
        cols = slice((at % half) * block, (at % half + 1) * block)
        cot = jnp.where(seq == at // half, cot_ref[:, cols], cot2_ref[:, cols])
        cots[:, at * near:(at + 1) * near] = dot(cot, place, 1, 1).astype(bf16)
    for copy in copies:
        copy.wait()
    part = dot(tok_ref[...], full[...], 1, 1)
    high = part.astype(bf16)
    left = part - high.astype(f32)
    mid = left.astype(bf16)
    low = (left - mid.astype(f32)).astype(bf16)
    for at in range(SPLIT[0]):
        moved = 0.0
        for piece in (high, mid, low):
            moved = moved + dot(piece[:, at * near:(at + 1) * near], place)
        cols = slice((at % half) * block, (at % half + 1) * block)
        which = jnp.where(seq == at // half, 0, 1)
        if before:
            moved = moved + before[0][which, :, cols]
        parts_ref[which, :, cols] = moved
    tile = 1024
    for t in range(width // tile):
        cols = slice(t * tile, (t + 1) * tile)
        total = dot(cots[...], full[:, cols])
        if before:
            total = total + before[1][:, cols]
        grad_ref[:, cols] = total


def pick_kernel(key_ref, got_ref, found_ref, got, sems):
    rows = key_ref.shape[0]
    count = sems.shape[0]
    step = found_ref.shape[1] // count
    tiles = [pl.ds(t * step, step) for t in range(count)]
    copies = fetch([(got_ref.at[:, c], got.at[:, c]) for c in tiles], sems)
    key = jnp.concatenate([key_ref[...] + g for g in range(GROUPS)], axis=0)
    pick = one(key == iota((GROUPS * rows, got.shape[0]), 1))
    for t in range(count):
        cols = slice(t * step, (t + 1) * step)
        copies[t].wait()
        found_ref[:, cols] = dot(pick, got[:, cols])


def finish_kernel(found_ref, base_ref, frozen_ref, bias_ref, grad_ref, proj_ref):
    tw = grad_ref.shape[1]
    grad_ref[...] = (base_ref[...] + found_ref[:, :tw]).astype(bf16)
    proj_ref[...] = (frozen_ref[...] + bias_ref[...] + found_ref[:, tw:]).astype(bf16)


def turn(value, shift):
    n = SPLIT[0]
    return lax.ppermute(value, "y", [(i, (i + shift) % n) for i in range(n)])


def swap(value, axis):
    return lax.ppermute(value, axis, [(0, 1), (1, 0)])


def on_device(tokens, weight, bias, adapter_down, adapter_up, cotangent, block_task, owner_slot):
    rows_dev, half_width = tokens.shape
    owners = OWNERS
    blocks_dev = block_task.shape[0]
    block_rows = rows_dev // blocks_dev
    task_dev, rank, key_part = adapter_up.shape
    chunk = block_rows * GROUPS
    sent_rows = owners * chunk
    tw, cw = half_width // GROUPS, key_part // GROUPS
    seq = lax.axis_index("seq")

    sent, code = pl.pallas_call(
        pack_kernel,
        out_shape=(
            jax.ShapeDtypeStruct((sent_rows, tw + cw + 128), bf16),
            jax.ShapeDtypeStruct((1, GROUPS * rows_dev), jnp.int32),
        ),
        in_specs=[VMEM] * 4,
        out_specs=(HBM, VMEM),
        scratch_shapes=[
            pltpu.VMEM((GROUPS * rows_dev, tw + cw + 128), bf16),
            pltpu.VMEM((sent_rows, tw + cw + 128), bf16),
            pltpu.SemaphoreType.DMA((4,)),
        ],
        compiler_params=WHOLE,
        name="pack",
    )(block_task[None, :], owner_slot[None, :], tokens, cotangent)
    other_cot = swap(cotangent, "seq")
    got = lax.all_to_all(sent, SUB, split_axis=0, concat_axis=0, tiled=True)

    slab = lax.all_gather(weight, ("z", "c"), axis=0).reshape(SPLIT[2], 2, -1, half_width)
    slab = lax.dynamic_index_in_dim(slab, lax.axis_index("c"), 1, keepdims=False)
    slab = slab.reshape(-1, half_width)
    slab = jnp.concatenate([slab, swap(slab, "xl")], axis=0)
    cut = half_width * 3 // 4
    whole = lax.all_gather(slab[:, :cut], "y", axis=0, tiled=True)
    own = [whole, slab[:, cut:]] + [turn(slab[:, cut:], shift) for shift in range(1, SPLIT[0])]

    down_t = adapter_down.transpose(1, 2, 0).reshape(task_dev * rank, half_width)
    up_t = adapter_up.reshape(task_dev * rank, key_part)
    owner_rows = owners * block_rows
    rows_in, cots_in, label_in = pl.pallas_call(
        rows_kernel,
        out_shape=(
            jax.ShapeDtypeStruct((owner_rows, half_width), bf16),
            jax.ShapeDtypeStruct((owner_rows, key_part), bf16),
            jax.ShapeDtypeStruct((owner_rows, 128), bf16),
        ),
        in_specs=[VMEM],
        out_specs=(VMEM,) * 3,
        compiler_params=PARAMS,
        name="owner_rows",
    )(got)
    low_mine = pl.pallas_call(
        functools.partial(low_kernel, task_dev),
        out_shape=jax.ShapeDtypeStruct((owner_rows, 2 * rank), f32),
        in_specs=[VMEM] * 5,
        out_specs=VMEM,
        compiler_params=PARAMS,
        name="owner_in",
    )(rows_in, cots_in, label_in, down_t, up_t)
    low_other = swap(low_mine, "seq")
    to_return = pl.pallas_call(
        lambda *refs: owner_out_kernel(task_dev, *refs),
        out_shape=jax.ShapeDtypeStruct((sent_rows, tw + cw), bf16),
        in_specs=[VMEM] * 5,
        out_specs=HBM,
        scratch_shapes=[
            pltpu.VMEM((owner_rows, half_width), bf16),
            pltpu.VMEM((owner_rows, key_part), bf16),
            pltpu.VMEM((sent_rows, tw + cw), bf16),
            pltpu.SemaphoreType.DMA((4,)),
        ],
        compiler_params=pltpu.CompilerParams(vmem_limit_bytes=50 * 1024 * 1024),
        name="owner_out",
    )(low_mine, low_other, label_in, down_t, up_t)
    to_return, _ = lax.optimization_barrier((to_return, own[1:]))
    returned = lax.all_to_all(to_return, SUB, split_axis=0, concat_axis=0, tiled=True)

    down_gradient, up_gradient = pl.pallas_call(
        lambda *refs: gradients_kernel(task_dev, *refs),
        out_shape=(
            jax.ShapeDtypeStruct((task_dev * rank, half_width), f32),
            jax.ShapeDtypeStruct((task_dev * rank, key_part), f32),
        ),
        in_specs=[VMEM] * 4,
        out_specs=(VMEM, VMEM),
        scratch_shapes=[
            pltpu.VMEM((owner_rows, half_width), bf16),
            pltpu.VMEM((owner_rows, key_part), bf16),
        ],
        compiler_params=PARAMS,
        name="gradients",
    )(got, low_mine, low_other, label_in)
    up_gradient = up_gradient.reshape(task_dev, rank, key_part)
    down_gradient = down_gradient.reshape(task_dev, rank, half_width).transpose(2, 0, 1)

    places = jnp.stack([lax.axis_index("y"), lax.axis_index("xl"), lax.axis_index("c"), seq])
    before = ()
    for flip, held in enumerate((own, [swap(part, "c") for part in own])):
        before = pl.pallas_call(
            functools.partial(base_kernel, flip),
            out_shape=(
                jax.ShapeDtypeStruct((2, rows_dev, key_part), f32),
                jax.ShapeDtypeStruct((rows_dev, half_width), f32),
            ),
            in_specs=[pl.BlockSpec(memory_space=pltpu.SMEM)]
            + [VMEM] * 3 + [HBM] * len(held) + [VMEM] * len(before),
            out_specs=(VMEM, VMEM),
            scratch_shapes=[
                pltpu.VMEM((key_part, half_width), bf16),
                pltpu.VMEM((rows_dev, key_part), bf16),
                pltpu.SemaphoreType.DMA((len(held),)),
            ],
            compiler_params=PARAMS,
            name=("base_own", "base_other")[flip],
        )(places.astype(jnp.int32), tokens, cotangent, other_cot, *held, *before)
    parts, base_grad = before
    frozen = parts[0] + swap(parts[1], "seq")

    row_key = code[0, :rows_dev]
    found = pl.pallas_call(
        pick_kernel,
        out_shape=jax.ShapeDtypeStruct((GROUPS * rows_dev, tw + cw), f32),
        in_specs=[VMEM, HBM],
        out_specs=VMEM,
        scratch_shapes=[
            pltpu.VMEM((sent_rows, tw + cw), bf16),
            pltpu.SemaphoreType.DMA((3,)),
        ],
        compiler_params=PARAMS,
        name="pick",
    )(row_key[:, None], returned)
    grad_tokens, projected = pl.pallas_call(
        finish_kernel,
        out_shape=(
            jax.ShapeDtypeStruct((rows_dev, half_width), bf16),
            jax.ShapeDtypeStruct((rows_dev, key_part), bf16),
        ),
        grid=(GROUPS,),
        in_specs=[
            pl.BlockSpec((rows_dev, tw + cw), lambda g: (g, 0)),
            pl.BlockSpec((rows_dev, tw), lambda g: (0, g)),
            pl.BlockSpec((rows_dev, cw), lambda g: (0, g)),
            pl.BlockSpec((1, cw), lambda g: (0, g)),
        ],
        out_specs=(
            pl.BlockSpec((rows_dev, tw), lambda g: (0, g)),
            pl.BlockSpec((rows_dev, cw), lambda g: (0, g)),
        ),
        compiler_params=PARAMS,
        name="finish",
    )(found, base_grad, frozen, bias[None, :])
    return (projected, grad_tokens, down_gradient, up_gradient)


def solution(mesh):
    fine = Mesh(mesh.devices.reshape(SPLIT + (mesh.shape["seq"],)), SUB + ("seq",))
    return jax.shard_map(
        on_device,
        mesh=fine,
        in_specs=(
            P(SUB, "seq"),
            P(SUB, "seq"),
            P("seq"),
            P("seq", SUB, None),
            P(SUB, None, "seq"),
            P(SUB, "seq"),
            P(SUB),
            P(),
        ),
        out_specs=(
            P(SUB, "seq"),
            P(SUB, "seq"),
            P("seq", SUB, None),
            P(SUB, None, "seq"),
        ),
        check_vma=False,
    )
```
